32 devices in a mesh: groups: 2 (over y), blk: 4 (over z), heads: 2 (over x), section: 2 (over core).
Axes of the slice: x: 2, y: 2, z: 4, core: 2. Of those that a mesh axis runs over, the one named last changes fastest.
Arguments:
- dec_states: bfloat16 [4096, 2304], P(('groups', 'blk', 'section')), parts along dimension 0, may hold values from -6 to 6
- cross_keys: bfloat16 [1024, 1, 256], P(('groups', 'blk')), parts along dimension 0, may hold values from -15 to 15
- cross_values: bfloat16 [1024, 1, 256], P(('groups', 'blk')), parts along dimension 0, may hold values from -6 to 6
- attn_gain: float32 [2304], replicated, may hold values from 0.1 to 1.9
- query_weight: bfloat16 [2304, 512], P(None, 'heads'), may hold values from -0.125 to 0.125
- out_weight: bfloat16 [512, 2304], P('heads'), may hold values from -0.25 to 0.25
- post_attn_gain: float32 [2304], replicated, may hold values from 0.1 to 1.9
- ffn_gain: float32 [2304], replicated, may hold values from 0.1 to 1.9
- gate_weight: bfloat16 [2304, 9216], P('blk', ('heads', 'section')), may hold values from -0.125 to 0.125
- up_weight: bfloat16 [2304, 9216], P('blk', ('heads', 'section')), may hold values from -0.125 to 0.125
- down_weight: bfloat16 [9216, 2304], P(('heads', 'section'), 'blk'), may hold values from -0.0625 to 0.0625
- post_ffn_gain: float32 [2304], replicated, may hold values from 0.1 to 1.9
Outputs:
- scored_states: bfloat16 [4096, 2304], P(('groups', 'blk', 'heads', 'section')), parts along dimension 0
The draws below stay inside these ranges and needn't reach their ends.
There are 2 independent parts, one for each index of `groups`. The reference program is written for one: setup_inputs(seed, part) draws one part's arguments, and reference() takes and returns one part's arrays. A program takes and returns all parts, laid end to end along the dimension named above; an argument that names none is the same for every part. Nothing has to cross between parts.
All inputs are finite; a program needn't handle non-finite values.
Results may differ from the reference program's by a relative error of at most 0.02.
Values may be sent and summed in bfloat16 or wider, within the bound.
A program may use at most 128 MiB of HBM per device.

```python
import jax
import jax.numpy as jnp
from jax import lax

D = 2304
FF = 9216
HD = 256
GROUP = 2
HEADS = 2
KVH = 1
TGT = 2048
SRC = 512
N_HEADS = 2
N_SECTION = 2


def level_of(rng, extent, pieces, least, largest):
    factor_of, own = 1.0, jax.random.fold_in(rng, 6)
    for axis_at, shards_of in pieces:
        steps = jnp.exp(jax.random.uniform(jax.random.fold_in(own, axis_at), (shards_of,), jnp.float32, least / len(pieces), largest / len(pieces)))
        factor_of = factor_of * jnp.repeat(steps, extent[axis_at] // shards_of).reshape([-1 if axis == axis_at else 1 for axis in range(len(extent))])
    return factor_of


def centred(own_key, dims, deviation, reach, pieces=(), kind=jnp.bfloat16):
    entries = jax.random.normal(own_key, dims, jnp.float32) * deviation
    if len(pieces) > 0:
        entries = level_of(own_key, dims, pieces, -0.22, 0.18) * entries
    return jnp.clip(entries, min=-reach, max=reach).astype(kind)


def setup_inputs(seed: int = 0, part: int = 0) -> dict:
    splits = jax.random.split(jax.random.key(seed), 13)
    part_splits = jax.random.split(jax.random.fold_in(splits[12], part), 13)
    return {
        "dec_states": centred(part_splits[0], (TGT, D), 1.0, 6.0, ((0, 8),)),
        "cross_keys": centred(part_splits[1], (SRC, KVH, HD), 2.5, 15.0, ((0, 4),)),
        "cross_values": centred(part_splits[2], (SRC, KVH, HD), 1.0, 6.0, ((0, 4),)),
        "attn_gain": jnp.clip(1.0 + 0.18 * jax.random.normal(splits[3], (D,), jnp.float32), 0.1, 1.9),
        "query_weight": centred(splits[4], (D, HEADS * HD), D ** -0.5, 0.125, ((1, 2),)),
        "out_weight": centred(splits[5], (HEADS * HD, D), (HEADS * HD) ** -0.5, 0.25, ((0, 2),)),
        "post_attn_gain": jnp.clip(1.0 + 0.18 * jax.random.normal(splits[6], (D,), jnp.float32), 0.1, 1.9),
        "ffn_gain": jnp.clip(1.0 + 0.18 * jax.random.normal(splits[7], (D,), jnp.float32), 0.1, 1.9),
        "gate_weight": centred(splits[8], (D, FF), D ** -0.5, 0.125, ((0, 4), (1, 4))),
        "up_weight": centred(splits[9], (D, FF), D ** -0.5, 0.125, ((0, 4), (1, 4))),
        "down_weight": centred(splits[10], (FF, D), FF ** -0.5, 0.0625, ((0, 4), (1, 4))),
        "post_ffn_gain": jnp.clip(1.0 + 0.18 * jax.random.normal(splits[11], (D,), jnp.float32), 0.1, 1.9),
    }


softcap_limit = 50.0

def rms_scale(values, gain):
    return values * lax.rsqrt(lax.optimization_barrier(jnp.mean(values * values, axis=-1, keepdims=True)) + 1e-06) * gain

def reference(dec_states, cross_keys, cross_values, attn_gain, query_weight, out_weight, post_attn_gain, ffn_gain, gate_weight, up_weight, down_weight, post_ffn_gain):
    states = dec_states.astype(jnp.float32)
    normed = rms_scale(states, attn_gain).astype(jnp.bfloat16)
    queries = jnp.dot(normed, query_weight, preferred_element_type=jnp.float32).astype(jnp.bfloat16)

    def head_step(total, head):
        head_queries = lax.dynamic_slice_in_dim(queries, head * HD, HD, 1)
        kv_index = head // GROUP
        keys = lax.dynamic_index_in_dim(cross_keys, kv_index, 1, keepdims=False)
        values = lax.dynamic_index_in_dim(cross_values, kv_index, 1, keepdims=False)
        raw = lax.dot_general(head_queries, keys, (((1,), (1,)), ((), ())), preferred_element_type=jnp.float32) * HD ** (-0.5)
        scores = softcap_limit * jnp.tanh(raw / softcap_limit)
        probs = jnp.exp(scores)
        totals = lax.optimization_barrier(jnp.sum(probs, axis=1, keepdims=True))
        context = (jnp.dot(probs.astype(jnp.bfloat16), values, preferred_element_type=jnp.float32) / totals).astype(jnp.bfloat16)
        out_rows = lax.dynamic_slice_in_dim(out_weight, head * HD, HD, 0)
        term = jnp.dot(context, out_rows, preferred_element_type=jnp.float32).astype(jnp.bfloat16)
        term = lax.optimization_barrier(term)
        return (total + term.astype(jnp.float32), None)
    attended, unused = lax.scan(head_step, jnp.zeros((TGT, D), jnp.float32), jnp.arange(HEADS, dtype=jnp.int32))
    residual = (states + rms_scale(attended, post_attn_gain)).astype(jnp.bfloat16)
    ffn_input = rms_scale(residual.astype(jnp.float32), ffn_gain).astype(jnp.bfloat16)
    group_count = N_HEADS * N_SECTION
    group_units = FF // group_count

    def group_step(total, group):
        start = group * group_units
        gate = jnp.dot(ffn_input, lax.dynamic_slice_in_dim(gate_weight, start, group_units, 1), preferred_element_type=jnp.float32)
        up_part = jnp.dot(ffn_input, lax.dynamic_slice_in_dim(up_weight, start, group_units, 1), preferred_element_type=jnp.float32)
        hidden = (jax.nn.gelu(gate, approximate=True) * up_part).astype(jnp.bfloat16)
        term = jnp.dot(hidden, lax.dynamic_slice_in_dim(down_weight, start, group_units, 0), preferred_element_type=jnp.float32).astype(jnp.bfloat16)
        term = lax.optimization_barrier(term)
        return (total + term.astype(jnp.float32), None)
    ffn_out, unused_two = lax.scan(group_step, jnp.zeros((TGT, D), jnp.float32), jnp.arange(group_count, dtype=jnp.int32))
    return (residual.astype(jnp.float32) + rms_scale(ffn_out, post_ffn_gain)).astype(jnp.bfloat16)
```

```python
import jax
import jax.numpy as jnp
from jax import lax
from jax.sharding import PartitionSpec as P

HD = 256
GROUP = 2


softcap_limit = 50.0


def from_partner(block, axis, bit):
    count = lax.axis_size(axis)
    route = []
    for low in range(count):
        high = low | 1 << bit
        if high != low and high < count:
            route += [(low, high), (high, low)]
    return lax.ppermute(block, axis, route)


def rms_scale(values, gain):
    return values * lax.rsqrt(jnp.mean(values * values, axis=-1, keepdims=True) + 1e-06) * gain


def capped_scores(queries, keys):
    raw = lax.dot_general(
        queries, keys, (((1,), (1,)), ((), ())), preferred_element_type=jnp.float32
    ) * HD ** (-0.5)
    return softcap_limit * jnp.tanh(raw / softcap_limit)


def reshard_over_blk(weight, split_axis, concat_axis):
    count = lax.axis_size("blk")
    groups = lax.axis_size("groups")
    me = lax.axis_index("blk")
    my_group = lax.axis_index("groups")
    piece = weight.shape[split_axis] // count
    depth = weight.shape[concat_axis]
    shape = [piece, piece]
    shape[concat_axis] = depth * count
    sizes = [piece, piece]
    sizes[concat_axis] = depth
    half = sizes[0] // groups
    whole = jnp.zeros(shape, weight.dtype)
    own = lax.dynamic_slice_in_dim(weight, me * piece, piece, split_axis)
    whole = lax.dynamic_update_slice_in_dim(whole, own, me * depth, concat_axis)
    for step in range(1, count):
        peer = me ^ step
        packet = lax.dynamic_slice_in_dim(weight, peer * piece, piece, split_axis)
        packet = lax.dynamic_slice_in_dim(packet, my_group * half, half, 0)
        first = lax.ppermute(packet, "blk", [(i, i ^ step) for i in range(count)])
        second = lax.ppermute(first, "groups", [(0, 1), (1, 0)])
        for part, group in ((first, my_group), (second, 1 - my_group)):
            at = [group * half, 0]
            at[concat_axis] += peer * depth
            whole = lax.dynamic_update_slice(whole, part, at)
    return whole


def weights_body(
    dec_states,
    cross_keys,
    cross_values,
    attn_gain,
    query_weight,
    out_weight,
    post_attn_gain,
    ffn_gain,
    gate_weight,
    up_weight,
    down_weight,
    post_ffn_gain,
):
    head_index = lax.axis_index("heads")
    kv_index = head_index // GROUP
    keys_local = lax.dynamic_index_in_dim(cross_keys, kv_index, 1, keepdims=False)
    values_local = lax.dynamic_index_in_dim(cross_values, kv_index, 1, keepdims=False)
    gate_full, up_full, down_full = (
        lax.all_gather(gate_weight, "blk", axis=0, tiled=True),
        lax.all_gather(up_weight, "blk", axis=0, tiled=True),
        lax.all_gather(down_weight, "blk", axis=1, tiled=True),
    )
    states = dec_states.astype(jnp.float32)
    normed = rms_scale(states, attn_gain).astype(jnp.bfloat16)
    queries = jnp.dot(normed, query_weight, preferred_element_type=jnp.float32).astype(jnp.bfloat16)
    rows_here = queries.shape[0]
    probs = jnp.exp(capped_scores(queries, lax.all_gather(keys_local, "blk", axis=0, tiled=True)))
    numer = jnp.dot(
        probs.astype(jnp.bfloat16),
        lax.all_gather(values_local, "blk", axis=0, tiled=True),
        preferred_element_type=jnp.float32,
    )
    numer, denom = (numer, jnp.sum(probs, axis=1))
    context = (numer / denom[:, None]).astype(jnp.bfloat16)
    head_term = jnp.dot(context, out_weight, preferred_element_type=jnp.float32)
    attended = lax.psum(head_term.astype(jnp.bfloat16), "heads").astype(jnp.float32)
    residual = (states + rms_scale(attended, post_attn_gain)).astype(jnp.bfloat16)
    ffn_input = rms_scale(residual.astype(jnp.float32), ffn_gain).astype(jnp.bfloat16)
    section_size = lax.axis_size("section")
    section_index = lax.axis_index("section")
    out_rows = rows_here // lax.axis_size("heads")
    block_index = head_index * section_size + section_index
    ffn_rows = lax.all_gather(ffn_input, "section", axis=0, tiled=True)
    partner_block = head_index * section_size + (1 - section_index)
    send_start = jnp.clip(
        partner_block * out_rows - section_index * rows_here, 0, rows_here - out_rows
    )
    outgoing = lax.dynamic_slice_in_dim(residual, send_start, out_rows, 0)
    incoming = from_partner(outgoing, "section", 0)
    own_start = jnp.clip(
        block_index * out_rows - section_index * rows_here, 0, rows_here - out_rows
    )
    local_rows = lax.dynamic_slice_in_dim(residual, own_start, out_rows, 0)
    holder = block_index * out_rows // rows_here
    residual_out = jnp.where(holder == section_index, local_rows, incoming)
    gate = jnp.dot(ffn_rows, gate_full, preferred_element_type=jnp.float32)
    up_part = jnp.dot(ffn_rows, up_full, preferred_element_type=jnp.float32)
    hidden = (jax.nn.gelu(gate, approximate=True) * up_part).astype(jnp.bfloat16)
    terms = jnp.dot(hidden, down_full, preferred_element_type=jnp.float32)
    ffn_out = lax.psum_scatter(
        terms.astype(jnp.bfloat16), ("heads", "section"), scatter_dimension=0, tiled=True
    ).astype(jnp.float32)
    return (residual_out.astype(jnp.float32) + rms_scale(ffn_out, post_ffn_gain)).astype(
        jnp.bfloat16
    )


def rows_body(
    dec_states,
    cross_keys,
    cross_values,
    attn_gain,
    query_weight,
    out_weight,
    post_attn_gain,
    ffn_gain,
    gate_weight,
    up_weight,
    down_weight,
    post_ffn_gain,
):
    head_index = lax.axis_index("heads")
    kv_index = head_index // GROUP
    keys_local = lax.dynamic_index_in_dim(cross_keys, kv_index, 1, keepdims=False)
    values_local = lax.dynamic_index_in_dim(cross_values, kv_index, 1, keepdims=False)
    kv_all = lax.all_gather(jnp.stack([keys_local, values_local]), "blk", axis=1, tiled=True)
    gate_mine = reshard_over_blk(gate_weight, 1, 0)
    up_mine = reshard_over_blk(up_weight, 1, 0)
    down_mine = reshard_over_blk(down_weight, 0, 1)
    states = dec_states.astype(jnp.float32)
    normed = rms_scale(states, attn_gain).astype(jnp.bfloat16)
    queries = jnp.dot(normed, query_weight, preferred_element_type=jnp.float32).astype(jnp.bfloat16)
    probs = jnp.exp(capped_scores(queries, kv_all[0]))
    numer = jnp.dot(probs.astype(jnp.bfloat16), kv_all[1], preferred_element_type=jnp.float32)
    denom = jnp.sum(probs, axis=1)
    context = (numer / denom[:, None]).astype(jnp.bfloat16)
    head_term = jnp.dot(context, out_weight, preferred_element_type=jnp.float32).astype(jnp.bfloat16)
    heads = lax.axis_size("heads")
    section_size = lax.axis_size("section")
    section_index = lax.axis_index("section")
    attended = lax.psum_scatter(head_term, "heads", scatter_dimension=0, tiled=True).astype(jnp.float32)
    out_rows = attended.shape[0]
    kept = lax.dynamic_slice_in_dim(dec_states, head_index * out_rows, out_rows, 0).astype(jnp.float32)
    residual = (kept + rms_scale(attended, post_attn_gain)).astype(jnp.bfloat16)
    ffn_input = rms_scale(residual.astype(jnp.float32), ffn_gain).astype(jnp.bfloat16)
    route = [
        (h * section_size + s, s * heads + h) for h in range(heads) for s in range(section_size)
    ]
    residual_out = lax.ppermute(residual, ("heads", "section"), route)
    ffn_rows = lax.all_gather(ffn_input, ("blk", "section", "heads"), axis=0, tiled=True)
    gate = jnp.dot(ffn_rows, gate_mine, preferred_element_type=jnp.float32)
    up_part = jnp.dot(ffn_rows, up_mine, preferred_element_type=jnp.float32)
    hidden = (jax.nn.gelu(gate, approximate=True) * up_part).astype(jnp.bfloat16)
    terms = jnp.dot(hidden, down_mine, preferred_element_type=jnp.float32).astype(jnp.bfloat16)
    ffn_out = lax.psum_scatter(
        terms, ("blk", "heads", "section"), scatter_dimension=0, tiled=True
    ).astype(jnp.float32)
    return (residual_out.astype(jnp.float32) + rms_scale(ffn_out, post_ffn_gain)).astype(
        jnp.bfloat16
    )


def rows_travel(mesh, dec_states, gate_weight):
    blk, heads, section, groups = (mesh.shape[a] for a in ("blk", "heads", "section", "groups"))
    width = dec_states.shape[1]
    rows = dec_states.shape[0] // groups
    units = gate_weight.shape[1] // (heads * section)
    gathered = 3 * width * units
    moved = 3 * width * units // blk + 2 * rows * width
    power = blk & (blk - 1) == 0
    fits = units % (blk * groups) == 0 and width % (blk * groups) == 0
    return groups == 2 and power and fits and moved < gathered


def solution(mesh):
    in_specs = (
        P(("groups", "blk", "section"), None),
        P(("groups", "blk"), None, None),
        P(("groups", "blk"), None, None),
        P(),
        P(None, "heads"),
        P("heads", None),
        P(),
        P(),
        P("blk", ("heads", "section")),
        P("blk", ("heads", "section")),
        P(("heads", "section"), "blk"),
        P(),
    )
    out_specs = P(("groups", "blk", "heads", "section"), None)

    def layer(*args):
        plan = rows_body if rows_travel(mesh, args[0], args[8]) else weights_body
        return jax.shard_map(
            plan, mesh=mesh, in_specs=in_specs, out_specs=out_specs, check_vma=False
        )(*args)

    return layer
```

```python
import jax
import jax.numpy as jnp
from jax import lax
from jax.sharding import PartitionSpec as P

HD = 256
GROUP = 2


softcap_limit = 50.0


def from_partner(block, axis, bit):
    count = lax.axis_size(axis)
    route = []
    for low in range(count):
        high = low | 1 << bit
        if high != low and high < count:
            route += [(low, high), (high, low)]
    return lax.ppermute(block, axis, route)


def rms_scale(values, gain):
    return values * lax.rsqrt(jnp.mean(values * values, axis=-1, keepdims=True) + 1e-06) * gain


def capped_scores(queries, keys):
    raw = lax.dot_general(
        queries, keys, (((1,), (1,)), ((), ())), preferred_element_type=jnp.float32
    ) * HD ** (-0.5)
    return softcap_limit * jnp.tanh(raw / softcap_limit)


def reshard_over_blk(weight, split_axis, concat_axis):
    count = lax.axis_size("blk")
    groups = lax.axis_size("groups")
    me = lax.axis_index("blk")
    my_group = lax.axis_index("groups")
    piece = weight.shape[split_axis] // count
    depth = weight.shape[concat_axis]
    sizes = [piece, piece]
    sizes[concat_axis] = depth
    half = sizes[0] // groups
    whole = jnp.zeros((count * sizes[0], sizes[1]), weight.dtype)
    own = lax.dynamic_slice_in_dim(weight, me * piece, piece, split_axis)
    whole = lax.dynamic_update_slice_in_dim(whole, own, me * sizes[0], 0)
    for step in range(1, count):
        peer = me ^ step
        packet = lax.dynamic_slice_in_dim(weight, peer * piece, piece, split_axis)
        packet = lax.dynamic_slice_in_dim(packet, my_group * half, half, 0)
        first = lax.ppermute(packet, "blk", [(i, i ^ step) for i in range(count)])
        second = lax.ppermute(first, "groups", [(0, 1), (1, 0)])
        for part, group in ((first, my_group), (second, 1 - my_group)):
            whole = lax.dynamic_update_slice_in_dim(whole, part, peer * sizes[0] + group * half, 0)
    if concat_axis == 1:
        whole = whole.reshape(count, *sizes).transpose(1, 0, 2).reshape(sizes[0], count * sizes[1])
    return whole


def weights_body(
    dec_states,
    cross_keys,
    cross_values,
    attn_gain,
    query_weight,
    out_weight,
    post_attn_gain,
    ffn_gain,
    gate_weight,
    up_weight,
    down_weight,
    post_ffn_gain,
):
    head_index = lax.axis_index("heads")
    kv_index = head_index // GROUP
    keys_local = lax.dynamic_index_in_dim(cross_keys, kv_index, 1, keepdims=False)
    values_local = lax.dynamic_index_in_dim(cross_values, kv_index, 1, keepdims=False)
    gate_full, up_full, down_full = (
        lax.all_gather(gate_weight, "blk", axis=0, tiled=True),
        lax.all_gather(up_weight, "blk", axis=0, tiled=True),
        lax.all_gather(down_weight, "blk", axis=1, tiled=True),
    )
    states = dec_states.astype(jnp.float32)
    normed = rms_scale(states, attn_gain).astype(jnp.bfloat16)
    queries = jnp.dot(normed, query_weight, preferred_element_type=jnp.float32).astype(jnp.bfloat16)
    rows_here = queries.shape[0]
    probs = jnp.exp(capped_scores(queries, lax.all_gather(keys_local, "blk", axis=0, tiled=True)))
    numer = jnp.dot(
        probs.astype(jnp.bfloat16),
        lax.all_gather(values_local, "blk", axis=0, tiled=True),
        preferred_element_type=jnp.float32,
    )
    numer, denom = (numer, jnp.sum(probs, axis=1))
    context = (numer / denom[:, None]).astype(jnp.bfloat16)
    head_term = jnp.dot(context, out_weight, preferred_element_type=jnp.float32)
    attended = lax.psum(head_term.astype(jnp.bfloat16), "heads").astype(jnp.float32)
    residual = (states + rms_scale(attended, post_attn_gain)).astype(jnp.bfloat16)
    ffn_input = rms_scale(residual.astype(jnp.float32), ffn_gain).astype(jnp.bfloat16)
    section_size = lax.axis_size("section")
    section_index = lax.axis_index("section")
    out_rows = rows_here // lax.axis_size("heads")
    block_index = head_index * section_size + section_index
    ffn_rows = lax.all_gather(ffn_input, "section", axis=0, tiled=True)
    partner_block = head_index * section_size + (1 - section_index)
    send_start = jnp.clip(
        partner_block * out_rows - section_index * rows_here, 0, rows_here - out_rows
    )
    outgoing = lax.dynamic_slice_in_dim(residual, send_start, out_rows, 0)
    incoming = from_partner(outgoing, "section", 0)
    own_start = jnp.clip(
        block_index * out_rows - section_index * rows_here, 0, rows_here - out_rows
    )
    local_rows = lax.dynamic_slice_in_dim(residual, own_start, out_rows, 0)
    holder = block_index * out_rows // rows_here
    residual_out = jnp.where(holder == section_index, local_rows, incoming)
    gate = jnp.dot(ffn_rows, gate_full, preferred_element_type=jnp.float32)
    up_part = jnp.dot(ffn_rows, up_full, preferred_element_type=jnp.float32)
    hidden = (jax.nn.gelu(gate, approximate=True) * up_part).astype(jnp.bfloat16)
    terms = jnp.dot(hidden, down_full, preferred_element_type=jnp.float32)
    ffn_out = lax.psum_scatter(
        terms.astype(jnp.bfloat16), ("heads", "section"), scatter_dimension=0, tiled=True
    ).astype(jnp.float32)
    return (residual_out.astype(jnp.float32) + rms_scale(ffn_out, post_ffn_gain)).astype(
        jnp.bfloat16
    )


def rows_body(
    dec_states,
    cross_keys,
    cross_values,
    attn_gain,
    query_weight,
    out_weight,
    post_attn_gain,
    ffn_gain,
    gate_weight,
    up_weight,
    down_weight,
    post_ffn_gain,
):
    head_index = lax.axis_index("heads")
    kv_index = head_index // GROUP
    keys_local = lax.dynamic_index_in_dim(cross_keys, kv_index, 1, keepdims=False)
    values_local = lax.dynamic_index_in_dim(cross_values, kv_index, 1, keepdims=False)
    kv_all = lax.all_gather(jnp.stack([keys_local, values_local]), "blk", axis=1, tiled=True)
    gate_mine = reshard_over_blk(gate_weight, 1, 0)
    up_mine = reshard_over_blk(up_weight, 1, 0)
    down_mine = reshard_over_blk(down_weight, 0, 1)
    states = dec_states.astype(jnp.float32)
    normed = rms_scale(states, attn_gain).astype(jnp.bfloat16)
    queries = jnp.dot(normed, query_weight, preferred_element_type=jnp.float32).astype(jnp.bfloat16)
    probs = jnp.exp(capped_scores(queries, kv_all[0]))
    numer = jnp.dot(probs.astype(jnp.bfloat16), kv_all[1], preferred_element_type=jnp.float32)
    denom = jnp.sum(probs, axis=1)
    context = (numer / denom[:, None]).astype(jnp.bfloat16)
    head_term = jnp.dot(context, out_weight, preferred_element_type=jnp.float32).astype(jnp.bfloat16)
    heads = lax.axis_size("heads")
    section_size = lax.axis_size("section")
    section_index = lax.axis_index("section")
    swap = [(0, 1), (1, 0)]
    out_rows = head_term.shape[0] // heads
    own_term = lax.dynamic_slice_in_dim(head_term, head_index * out_rows, out_rows, 0)
    sent_term = lax.dynamic_slice_in_dim(head_term, (1 - head_index) * out_rows, out_rows, 0)
    other_term = lax.ppermute(sent_term, "heads", swap)
    attended = own_term.astype(jnp.float32) + other_term.astype(jnp.float32)
    kept = lax.dynamic_slice_in_dim(dec_states, head_index * out_rows, out_rows, 0).astype(jnp.float32)
    residual = (kept + rms_scale(attended, post_attn_gain)).astype(jnp.bfloat16)
    ffn_input = rms_scale(residual.astype(jnp.float32), ffn_gain).astype(jnp.bfloat16)
    route = [
        (h * section_size + s, s * heads + h) for h in range(heads) for s in range(section_size)
    ]
    residual_out = lax.ppermute(residual, ("heads", "section"), route)
    near = lax.all_gather(ffn_input, "blk", axis=0, tiled=True)
    block_rows = near.shape[0]
    mine = jnp.concatenate([near, lax.ppermute(near, "heads", swap)])
    other = lax.ppermute(mine, "section", swap)
    send_mine = section_index != head_index
    kept_half = (section_index ^ head_index) * block_rows
    sent_half = block_rows - kept_half

    def summed_rows(rows):
        gate = jnp.dot(rows, gate_mine, preferred_element_type=jnp.float32)
        up_part = jnp.dot(rows, up_mine, preferred_element_type=jnp.float32)
        hidden = (jax.nn.gelu(gate, approximate=True) * up_part).astype(jnp.bfloat16)
        terms = jnp.dot(hidden, down_mine, preferred_element_type=jnp.float32).astype(jnp.bfloat16)
        away = lax.ppermute(
            lax.dynamic_slice_in_dim(terms, sent_half, block_rows, 0), "section", swap
        )
        here = lax.dynamic_slice_in_dim(terms, kept_half, block_rows, 0)
        return here.astype(jnp.float32) + away.astype(jnp.float32)

    first_sum = summed_rows(jnp.where(send_mine, mine, other)).astype(jnp.bfloat16)
    arrived = lax.ppermute(first_sum, "heads", swap)
    second_sum = summed_rows(jnp.where(send_mine, other, mine))
    chip_sum = (second_sum + arrived.astype(jnp.float32)).astype(jnp.bfloat16)
    ffn_out = lax.psum_scatter(chip_sum, "blk", scatter_dimension=0, tiled=True).astype(jnp.float32)
    return (residual_out.astype(jnp.float32) + rms_scale(ffn_out, post_ffn_gain)).astype(
        jnp.bfloat16
    )


def rows_travel(mesh, dec_states, gate_weight):
    blk, heads, section, groups = (mesh.shape[a] for a in ("blk", "heads", "section", "groups"))
    width = dec_states.shape[1]
    rows = dec_states.shape[0] // groups
    units = gate_weight.shape[1] // (heads * section)
    gathered = 3 * width * units
    moved = 3 * width * units // blk + 2 * rows * width
    power = blk & (blk - 1) == 0
    fits = units % (blk * groups) == 0 and width % (blk * groups) == 0
    pairs = groups == 2 and heads == 2 and section == 2
    return pairs and power and fits and moved < gathered


def solution(mesh):
    in_specs = (
        P(("groups", "blk", "section"), None),
        P(("groups", "blk"), None, None),
        P(("groups", "blk"), None, None),
        P(),
        P(None, "heads"),
        P("heads", None),
        P(),
        P(),
        P("blk", ("heads", "section")),
        P("blk", ("heads", "section")),
        P(("heads", "section"), "blk"),
        P(),
    )
    out_specs = P(("groups", "blk", "heads", "section"), None)

    def layer(*args):
        plan = rows_body if rows_travel(mesh, args[0], args[8]) else weights_body
        return jax.shard_map(
            plan, mesh=mesh, in_specs=in_specs, out_specs=out_specs, check_vma=False
        )(*args)

    return layer
```

```python
import jax
import jax.numpy as jnp
from jax import lax
from jax.sharding import PartitionSpec as P

HD = 256
GROUP = 2


softcap_limit = 50.0


def from_partner(block, axis, bit):
    count = lax.axis_size(axis)
    route = []
    for low in range(count):
        high = low | 1 << bit
        if high != low and high < count:
            route += [(low, high), (high, low)]
    return lax.ppermute(block, axis, route)


def rms_scale(values, gain):
    return values * lax.rsqrt(jnp.mean(values * values, axis=-1, keepdims=True) + 1e-06) * gain


def capped_scores(queries, keys):
    raw = lax.dot_general(
        queries, keys, (((1,), (1,)), ((), ())), preferred_element_type=jnp.float32
    ) * HD ** (-0.5)
    return softcap_limit * jnp.tanh(raw / softcap_limit)


def reshard_over_blk(weight, split_axis, concat_axis):
    count = lax.axis_size("blk")
    groups = lax.axis_size("groups")
    me = lax.axis_index("blk")
    my_group = lax.axis_index("groups")
    piece = weight.shape[split_axis] // count
    depth = weight.shape[concat_axis]
    sizes = [piece, piece]
    sizes[concat_axis] = depth
    half = sizes[0] // groups
    whole = jnp.zeros((count * sizes[0], sizes[1]), weight.dtype)
    own = lax.dynamic_slice_in_dim(weight, me * piece, piece, split_axis)
    whole = lax.dynamic_update_slice_in_dim(whole, own, me * sizes[0], 0)
    for step in range(1, count):
        peer = me ^ step
        packet = lax.dynamic_slice_in_dim(weight, peer * piece, piece, split_axis)
        packet = lax.dynamic_slice_in_dim(packet, my_group * half, half, 0)
        first = lax.ppermute(packet, "blk", [(i, i ^ step) for i in range(count)])
        second = lax.ppermute(first, "groups", [(0, 1), (1, 0)])
        for part, group in ((first, my_group), (second, 1 - my_group)):
            whole = lax.dynamic_update_slice_in_dim(whole, part, peer * sizes[0] + group * half, 0)
    if concat_axis == 1:
        whole = whole.reshape(count, *sizes).transpose(1, 0, 2).reshape(sizes[0], count * sizes[1])
    return whole


def weights_body(
    dec_states,
    cross_keys,
    cross_values,
    attn_gain,
    query_weight,
    out_weight,
    post_attn_gain,
    ffn_gain,
    gate_weight,
    up_weight,
    down_weight,
    post_ffn_gain,
):
    head_index = lax.axis_index("heads")
    kv_index = head_index // GROUP
    keys_local = lax.dynamic_index_in_dim(cross_keys, kv_index, 1, keepdims=False)
    values_local = lax.dynamic_index_in_dim(cross_values, kv_index, 1, keepdims=False)
    gate_full, up_full, down_full = (
        lax.all_gather(gate_weight, "blk", axis=0, tiled=True),
        lax.all_gather(up_weight, "blk", axis=0, tiled=True),
        lax.all_gather(down_weight, "blk", axis=1, tiled=True),
    )
    states = dec_states.astype(jnp.float32)
    normed = rms_scale(states, attn_gain).astype(jnp.bfloat16)
    queries = jnp.dot(normed, query_weight, preferred_element_type=jnp.float32).astype(jnp.bfloat16)
    rows_here = queries.shape[0]
    probs = jnp.exp(capped_scores(queries, lax.all_gather(keys_local, "blk", axis=0, tiled=True)))
    numer = jnp.dot(
        probs.astype(jnp.bfloat16),
        lax.all_gather(values_local, "blk", axis=0, tiled=True),
        preferred_element_type=jnp.float32,
    )
    numer, denom = (numer, jnp.sum(probs, axis=1))
    context = (numer / denom[:, None]).astype(jnp.bfloat16)
    head_term = jnp.dot(context, out_weight, preferred_element_type=jnp.float32)
    attended = lax.psum(head_term.astype(jnp.bfloat16), "heads").astype(jnp.float32)
    residual = (states + rms_scale(attended, post_attn_gain)).astype(jnp.bfloat16)
    ffn_input = rms_scale(residual.astype(jnp.float32), ffn_gain).astype(jnp.bfloat16)
    section_size = lax.axis_size("section")
    section_index = lax.axis_index("section")
    out_rows = rows_here // lax.axis_size("heads")
    block_index = head_index * section_size + section_index
    ffn_rows = lax.all_gather(ffn_input, "section", axis=0, tiled=True)
    partner_block = head_index * section_size + (1 - section_index)
    send_start = jnp.clip(
        partner_block * out_rows - section_index * rows_here, 0, rows_here - out_rows
    )
    outgoing = lax.dynamic_slice_in_dim(residual, send_start, out_rows, 0)
    incoming = from_partner(outgoing, "section", 0)
    own_start = jnp.clip(
        block_index * out_rows - section_index * rows_here, 0, rows_here - out_rows
    )
    local_rows = lax.dynamic_slice_in_dim(residual, own_start, out_rows, 0)
    holder = block_index * out_rows // rows_here
    residual_out = jnp.where(holder == section_index, local_rows, incoming)
    gate = jnp.dot(ffn_rows, gate_full, preferred_element_type=jnp.float32)
    up_part = jnp.dot(ffn_rows, up_full, preferred_element_type=jnp.float32)
    hidden = (jax.nn.gelu(gate, approximate=True) * up_part).astype(jnp.bfloat16)
    terms = jnp.dot(hidden, down_full, preferred_element_type=jnp.float32)
    ffn_out = lax.psum_scatter(
        terms.astype(jnp.bfloat16), ("heads", "section"), scatter_dimension=0, tiled=True
    ).astype(jnp.float32)
    return (residual_out.astype(jnp.float32) + rms_scale(ffn_out, post_ffn_gain)).astype(
        jnp.bfloat16
    )


def rows_body(
    dec_states,
    cross_keys,
    cross_values,
    attn_gain,
    query_weight,
    out_weight,
    post_attn_gain,
    ffn_gain,
    gate_weight,
    up_weight,
    down_weight,
    post_ffn_gain,
):
    head_index = lax.axis_index("heads")
    kv_index = head_index // GROUP
    keys_local = lax.dynamic_index_in_dim(cross_keys, kv_index, 1, keepdims=False)
    values_local = lax.dynamic_index_in_dim(cross_values, kv_index, 1, keepdims=False)
    kv_all = lax.all_gather(jnp.stack([keys_local, values_local]), "blk", axis=1, tiled=True)
    gate_mine = reshard_over_blk(gate_weight, 1, 0)
    up_mine = reshard_over_blk(up_weight, 1, 0)
    down_mine = reshard_over_blk(down_weight, 0, 1)
    states = dec_states.astype(jnp.float32)
    normed = rms_scale(states, attn_gain).astype(jnp.bfloat16)
    queries = jnp.dot(normed, query_weight, preferred_element_type=jnp.float32).astype(jnp.bfloat16)
    probs = jnp.exp(capped_scores(queries, kv_all[0]))
    numer = jnp.dot(probs.astype(jnp.bfloat16), kv_all[1], preferred_element_type=jnp.float32)
    denom = jnp.sum(probs, axis=1)
    context = (numer / denom[:, None]).astype(jnp.bfloat16)
    head_term = jnp.dot(context, out_weight, preferred_element_type=jnp.float32).astype(jnp.bfloat16)
    heads = lax.axis_size("heads")
    section_size = lax.axis_size("section")
    section_index = lax.axis_index("section")
    swap = [(0, 1), (1, 0)]
    out_rows = head_term.shape[0] // heads
    own_term = lax.dynamic_slice_in_dim(head_term, head_index * out_rows, out_rows, 0)
    sent_term = lax.dynamic_slice_in_dim(head_term, (1 - head_index) * out_rows, out_rows, 0)
    other_term = lax.ppermute(sent_term, "heads", swap)
    attended = own_term.astype(jnp.float32) + other_term.astype(jnp.float32)
    kept = lax.dynamic_slice_in_dim(dec_states, head_index * out_rows, out_rows, 0).astype(jnp.float32)
    residual = (kept + rms_scale(attended, post_attn_gain)).astype(jnp.bfloat16)
    ffn_input = rms_scale(residual.astype(jnp.float32), ffn_gain).astype(jnp.bfloat16)
    route = [
        (h * section_size + s, s * heads + h) for h in range(heads) for s in range(section_size)
    ]
    residual_out = lax.ppermute(residual, ("heads", "section"), route)
    ffn_rows = lax.all_gather(ffn_input, ("blk", "section", "heads"), axis=0, tiled=True)
    gate = jnp.dot(ffn_rows, gate_mine, preferred_element_type=jnp.float32)
    up_part = jnp.dot(ffn_rows, up_mine, preferred_element_type=jnp.float32)
    hidden = (jax.nn.gelu(gate, approximate=True) * up_part).astype(jnp.bfloat16)
    terms = jnp.dot(hidden, down_mine, preferred_element_type=jnp.float32).astype(jnp.bfloat16)
    ffn_out = lax.psum_scatter(
        terms, ("blk", "heads", "section"), scatter_dimension=0, tiled=True
    ).astype(jnp.float32)
    return (residual_out.astype(jnp.float32) + rms_scale(ffn_out, post_ffn_gain)).astype(
        jnp.bfloat16
    )


def rows_travel(mesh, dec_states, gate_weight):
    blk, heads, section, groups = (mesh.shape[a] for a in ("blk", "heads", "section", "groups"))
    width = dec_states.shape[1]
    rows = dec_states.shape[0] // groups
    units = gate_weight.shape[1] // (heads * section)
    gathered = 3 * width * units
    moved = 3 * width * units // blk + 2 * rows * width
    power = blk & (blk - 1) == 0
    fits = units % (blk * groups) == 0 and width % (blk * groups) == 0
    pairs = groups == 2 and heads == 2 and section == 2
    return pairs and power and fits and moved < gathered


def solution(mesh):
    in_specs = (
        P(("groups", "blk", "section"), None),
        P(("groups", "blk"), None, None),
        P(("groups", "blk"), None, None),
        P(),
        P(None, "heads"),
        P("heads", None),
        P(),
        P(),
        P("blk", ("heads", "section")),
        P("blk", ("heads", "section")),
        P(("heads", "section"), "blk"),
        P(),
    )
    out_specs = P(("groups", "blk", "heads", "section"), None)

    def layer(*args):
        plan = rows_body if rows_travel(mesh, args[0], args[8]) else weights_body
        return jax.shard_map(
            plan, mesh=mesh, in_specs=in_specs, out_specs=out_specs, check_vma=False
        )(*args)

    return layer
```

```python
import jax
import jax.numpy as jnp
from jax import lax
from jax.sharding import PartitionSpec as P

HD = 256
GROUP = 2


softcap_limit = 50.0


def from_partner(block, axis, bit):
    count = lax.axis_size(axis)
    route = []
    for low in range(count):
        high = low | 1 << bit
        if high != low and high < count:
            route += [(low, high), (high, low)]
    return lax.ppermute(block, axis, route)


def rms_scale(values, gain):
    return values * lax.rsqrt(jnp.mean(values * values, axis=-1, keepdims=True) + 1e-06) * gain


def capped_scores(queries, keys):
    raw = lax.dot_general(
        queries, keys, (((1,), (1,)), ((), ())), preferred_element_type=jnp.float32
    ) * HD ** (-0.5)
    return softcap_limit * jnp.tanh(raw / softcap_limit)


def reshard_over_blk(weight, split_axis, concat_axis):
    count = lax.axis_size("blk")
    groups = lax.axis_size("groups")
    me = lax.axis_index("blk")
    my_group = lax.axis_index("groups")
    piece = weight.shape[split_axis] // count
    depth = weight.shape[concat_axis]
    sizes = [piece, piece]
    sizes[concat_axis] = depth
    half = sizes[0] // groups
    whole = jnp.zeros((count * sizes[0], sizes[1]), weight.dtype)
    own = lax.dynamic_slice_in_dim(weight, me * piece, piece, split_axis)
    whole = lax.dynamic_update_slice_in_dim(whole, own, me * sizes[0], 0)
    for step in range(1, count):
        peer = me ^ step
        packet = lax.dynamic_slice_in_dim(weight, peer * piece, piece, split_axis)
        packet = lax.dynamic_slice_in_dim(packet, my_group * half, half, 0)
        first = lax.ppermute(packet, "blk", [(i, i ^ step) for i in range(count)])
        second = lax.ppermute(first, "groups", [(0, 1), (1, 0)])
        for part, group in ((first, my_group), (second, 1 - my_group)):
            whole = lax.dynamic_update_slice_in_dim(whole, part, peer * sizes[0] + group * half, 0)
    if concat_axis == 1:
        whole = whole.reshape(count, *sizes).transpose(1, 0, 2).reshape(sizes[0], count * sizes[1])
    return whole


def weights_body(
    dec_states,
    cross_keys,
    cross_values,
    attn_gain,
    query_weight,
    out_weight,
    post_attn_gain,
    ffn_gain,
    gate_weight,
    up_weight,
    down_weight,
    post_ffn_gain,
):
    head_index = lax.axis_index("heads")
    kv_index = head_index // GROUP
    keys_local = lax.dynamic_index_in_dim(cross_keys, kv_index, 1, keepdims=False)
    values_local = lax.dynamic_index_in_dim(cross_values, kv_index, 1, keepdims=False)
    gate_full, up_full, down_full = (
        lax.all_gather(gate_weight, "blk", axis=0, tiled=True),
        lax.all_gather(up_weight, "blk", axis=0, tiled=True),
        lax.all_gather(down_weight, "blk", axis=1, tiled=True),
    )
    states = dec_states.astype(jnp.float32)
    normed = rms_scale(states, attn_gain).astype(jnp.bfloat16)
    queries = jnp.dot(normed, query_weight, preferred_element_type=jnp.float32).astype(jnp.bfloat16)
    rows_here = queries.shape[0]
    probs = jnp.exp(capped_scores(queries, lax.all_gather(keys_local, "blk", axis=0, tiled=True)))
    numer = jnp.dot(
        probs.astype(jnp.bfloat16),
        lax.all_gather(values_local, "blk", axis=0, tiled=True),
        preferred_element_type=jnp.float32,
    )
    numer, denom = (numer, jnp.sum(probs, axis=1))
    context = (numer / denom[:, None]).astype(jnp.bfloat16)
    head_term = jnp.dot(context, out_weight, preferred_element_type=jnp.float32)
    attended = lax.psum(head_term.astype(jnp.bfloat16), "heads").astype(jnp.float32)
    residual = (states + rms_scale(attended, post_attn_gain)).astype(jnp.bfloat16)
    ffn_input = rms_scale(residual.astype(jnp.float32), ffn_gain).astype(jnp.bfloat16)
    section_size = lax.axis_size("section")
    section_index = lax.axis_index("section")
    out_rows = rows_here // lax.axis_size("heads")
    block_index = head_index * section_size + section_index
    ffn_rows = lax.all_gather(ffn_input, "section", axis=0, tiled=True)
    partner_block = head_index * section_size + (1 - section_index)
    send_start = jnp.clip(
        partner_block * out_rows - section_index * rows_here, 0, rows_here - out_rows
    )
    outgoing = lax.dynamic_slice_in_dim(residual, send_start, out_rows, 0)
    incoming = from_partner(outgoing, "section", 0)
    own_start = jnp.clip(
        block_index * out_rows - section_index * rows_here, 0, rows_here - out_rows
    )
    local_rows = lax.dynamic_slice_in_dim(residual, own_start, out_rows, 0)
    holder = block_index * out_rows // rows_here
    residual_out = jnp.where(holder == section_index, local_rows, incoming)
    gate = jnp.dot(ffn_rows, gate_full, preferred_element_type=jnp.float32)
    up_part = jnp.dot(ffn_rows, up_full, preferred_element_type=jnp.float32)
    hidden = (jax.nn.gelu(gate, approximate=True) * up_part).astype(jnp.bfloat16)
    terms = jnp.dot(hidden, down_full, preferred_element_type=jnp.float32)
    ffn_out = lax.psum_scatter(
        terms.astype(jnp.bfloat16), ("heads", "section"), scatter_dimension=0, tiled=True
    ).astype(jnp.float32)
    return (residual_out.astype(jnp.float32) + rms_scale(ffn_out, post_ffn_gain)).astype(
        jnp.bfloat16
    )


def rows_body(
    dec_states,
    cross_keys,
    cross_values,
    attn_gain,
    query_weight,
    out_weight,
    post_attn_gain,
    ffn_gain,
    gate_weight,
    up_weight,
    down_weight,
    post_ffn_gain,
):
    head_index = lax.axis_index("heads")
    kv_index = head_index // GROUP
    keys_local = lax.dynamic_index_in_dim(cross_keys, kv_index, 1, keepdims=False)
    values_local = lax.dynamic_index_in_dim(cross_values, kv_index, 1, keepdims=False)
    kv_all = lax.all_gather(jnp.stack([keys_local, values_local]), "blk", axis=1, tiled=True)
    gate_mine = reshard_over_blk(gate_weight, 1, 0)
    up_mine = reshard_over_blk(up_weight, 1, 0)
    down_mine = reshard_over_blk(down_weight, 0, 1)
    states = dec_states.astype(jnp.float32)
    normed = rms_scale(states, attn_gain).astype(jnp.bfloat16)
    queries = jnp.dot(normed, query_weight, preferred_element_type=jnp.float32).astype(jnp.bfloat16)
    probs = jnp.exp(capped_scores(queries, kv_all[0]))
    numer = jnp.dot(probs.astype(jnp.bfloat16), kv_all[1], preferred_element_type=jnp.float32)
    denom = jnp.sum(probs, axis=1)
    context = (numer / denom[:, None]).astype(jnp.bfloat16)
    head_term = jnp.dot(context, out_weight, preferred_element_type=jnp.float32).astype(jnp.bfloat16)
    heads = lax.axis_size("heads")
    section_size = lax.axis_size("section")
    section_index = lax.axis_index("section")
    swap = [(0, 1), (1, 0)]
    out_rows = head_term.shape[0] // heads
    own_term = lax.dynamic_slice_in_dim(head_term, head_index * out_rows, out_rows, 0)
    sent_term = lax.dynamic_slice_in_dim(head_term, (1 - head_index) * out_rows, out_rows, 0)
    other_term = lax.ppermute(sent_term, "heads", swap)
    attended = own_term.astype(jnp.float32) + other_term.astype(jnp.float32)
    kept = lax.dynamic_slice_in_dim(dec_states, head_index * out_rows, out_rows, 0).astype(jnp.float32)
    residual = (kept + rms_scale(attended, post_attn_gain)).astype(jnp.bfloat16)
    ffn_input = rms_scale(residual.astype(jnp.float32), ffn_gain).astype(jnp.bfloat16)
    route = [
        (h * section_size + s, s * heads + h) for h in range(heads) for s in range(section_size)
    ]
    residual_out = lax.ppermute(residual, ("heads", "section"), route)
    ffn_rows = lax.all_gather(ffn_input, ("blk", "section", "heads"), axis=0, tiled=True)
    gate = jnp.dot(ffn_rows, gate_mine, preferred_element_type=jnp.float32)
    up_part = jnp.dot(ffn_rows, up_mine, preferred_element_type=jnp.float32)
    hidden = (jax.nn.gelu(gate, approximate=True) * up_part).astype(jnp.bfloat16)
    terms = jnp.dot(hidden, down_mine, preferred_element_type=jnp.float32).astype(jnp.bfloat16)
    by_section = terms.reshape(-1, section_size, out_rows, terms.shape[1])
    kept_terms = lax.dynamic_index_in_dim(by_section, section_index, 1, keepdims=False)
    sent_terms = lax.dynamic_index_in_dim(by_section, 1 - section_index, 1, keepdims=False)
    came_terms = lax.ppermute(sent_terms, "section", swap)
    chip_sum = (kept_terms.astype(jnp.float32) + came_terms.astype(jnp.float32)).astype(jnp.bfloat16)
    ffn_out = lax.psum_scatter(
        chip_sum.reshape(-1, terms.shape[1]), ("blk", "heads"), scatter_dimension=0, tiled=True
    ).astype(jnp.float32)
    return (residual_out.astype(jnp.float32) + rms_scale(ffn_out, post_ffn_gain)).astype(
        jnp.bfloat16
    )


def rows_travel(mesh, dec_states, gate_weight):
    blk, heads, section, groups = (mesh.shape[a] for a in ("blk", "heads", "section", "groups"))
    width = dec_states.shape[1]
    rows = dec_states.shape[0] // groups
    units = gate_weight.shape[1] // (heads * section)
    gathered = 3 * width * units
    moved = 3 * width * units // blk + 2 * rows * width
    power = blk & (blk - 1) == 0
    fits = units % (blk * groups) == 0 and width % (blk * groups) == 0
    pairs = groups == 2 and heads == 2 and section == 2
    return pairs and power and fits and moved < gathered


def solution(mesh):
    in_specs = (
        P(("groups", "blk", "section"), None),
        P(("groups", "blk"), None, None),
        P(("groups", "blk"), None, None),
        P(),
        P(None, "heads"),
        P("heads", None),
        P(),
        P(),
        P("blk", ("heads", "section")),
        P("blk", ("heads", "section")),
        P(("heads", "section"), "blk"),
        P(),
    )
    out_specs = P(("groups", "blk", "heads", "section"), None)

    def layer(*args):
        plan = rows_body if rows_travel(mesh, args[0], args[8]) else weights_body
        return jax.shard_map(
            plan, mesh=mesh, in_specs=in_specs, out_specs=out_specs, check_vma=False
        )(*args)

    return layer
```
